32 devices in a mesh: seg: 8 (over z, core), lon: 4 (over y, x).
Axes of the slice: x: 2, y: 2, z: 4, core: 2. Of those that a mesh axis runs over, the one named last changes fastest.
Arguments:
- states: float32 [16, 16, 96, 1024], P('seg', None, 'lon'), may hold values from -20 to 20
- step_counts: int32 [16], replicated, may hold values from 4 to 6, as said below
- land: int32 [96, 1024], P('lon'), may hold values 0 or 1
- east_flow: float32 [96, 1024], P('lon'), may hold values from -0.15 to 0.15
- vert_mix: float32 [16], replicated, may hold values from 0.03 to 0.12
- coupling: float32 [16, 16], replicated, may hold values from -1.5 to 1.5
- amplitude: float32 [16, 16], replicated, may hold values from -4 to 4
- pattern: float32 [16, 96, 1024], P(None, 'lon'), may hold values from -5 to 5
Outputs:
- scaled: float32 [16, 16, 96, 1024], P('seg', None, 'lon')
- mismatch: float32 [], replicated
The draws below stay inside these ranges and needn't reach their ends.
Inputs may be any that keep to these rules, and one draw needn't show every extreme that they name: `step_counts`: some segment takes 6 steps.
All inputs are finite; a program needn't handle non-finite values. No bound on the sum of `land` on one device may be relied on, other than what follows from the above.
Results may differ from the reference program's by a relative error of at most 0.0075.
Values sent between devices are 32-bit elements; how exact they have to be, the bound alone decides.
No kernel may reach another device: no remote copies, remote signals or barrier semaphores. Data moves between devices by JAX's collectives and lax.ppermute only.
A program may use at most 64 MiB of HBM per device.

```python
import math
import jax
import jax.numpy as jnp
from jax import lax

TRACERS = 16
STEPS = 6
DEPTH = 16
COLS = 1024
SEGS = 16
NLON = 96


def draw_states(key, part):
    first, second = jax.random.split(jax.random.fold_in(key, 11))
    shape = (SEGS, TRACERS, NLON, COLS)
    place = jnp.arange(NLON, dtype=jnp.float32) / max(NLON - 1, 1)
    rising = jnp.exp(math.log(3.0) * place)[None, None, :, None]
    order = jnp.arange(SEGS, dtype=jnp.float32) / max(SEGS - 1, 1)
    rough = jnp.exp(jax.random.uniform(second, shape, jnp.float32, -0.35, 0.35))
    yearly = jnp.exp(math.log(3.0) * (order - 0.5))[:, None, None, None]
    base = jax.random.truncated_normal(first, -2.5, 2.5, shape, jnp.float32)
    return (base * rough * rising * yearly).astype(jnp.float32)


def draw_step_counts(key, part):
    first, second = jax.random.split(jax.random.fold_in(key, 23))
    counts = jax.random.randint(first, (SEGS,), STEPS - 2, STEPS + 1)
    chosen = jax.random.randint(second, (), 0, SEGS)
    return jnp.where(jnp.arange(SEGS) == chosen, STEPS, counts).astype(jnp.int32)


def set_ends(array, rng, low, high):
    extent = array.shape
    spot = [jax.random.randint(jax.random.fold_in(rng, axis), (), 0, extent[axis]) for axis in range(len(extent))]
    array = array.at[tuple(spot)].set(low)
    longest = extent.index(max(extent))
    spot[longest] = (spot[longest] + 1) % extent[longest]
    return array.at[tuple(spot)].set(high)


def level_of(own_key, dims, cuts, least, top_value):
    loudness = 1.0
    for dim, blocks in cuts:
        draws = jax.random.uniform(jax.random.fold_in(jax.random.fold_in(own_key, 6), dim), (blocks,), jnp.float32, least / len(cuts), top_value / len(cuts))
        loudness = loudness * jnp.repeat(jnp.exp(draws), dims[dim] // blocks).reshape((-1,) + (1,) * (len(dims) - 1 - dim))
    return loudness


def centred(own_key, extent, deviation, most, pieces=(), kind=jnp.bfloat16):
    values = deviation * jax.random.normal(own_key, extent, jnp.float32)
    if pieces:
        values = values * level_of(own_key, extent, pieces, -0.22, 0.18)
    return jnp.clip(values, -most, most).astype(kind)


def setup_inputs(seed: int = 0) -> dict:
    arg_keys = jax.random.split(jax.random.key(seed), 9)
    states = draw_states(jax.random.fold_in(arg_keys[8], 71), 0)
    step_counts = draw_step_counts(jax.random.fold_in(arg_keys[8], 71), 0)
    land = set_ends((jax.random.randint(arg_keys[2], (NLON, COLS), 0, 10) < 9).astype(jnp.int32), jax.random.fold_in(arg_keys[2], 1), 0, 1)
    east_flow = jnp.clip(jax.random.uniform(arg_keys[3], (NLON, COLS), jnp.float32, -0.15, 0.15) * level_of(arg_keys[3], (NLON, COLS), ((0, 4),), -0.4, 0.0), -0.15, 0.15)
    vert_mix = jnp.clip(jnp.exp(jax.random.uniform(arg_keys[4], (TRACERS,), jnp.float32, math.log(0.03), math.log(0.12))), 0.03, 0.12)
    coupling = centred(arg_keys[5], (TRACERS, TRACERS), 0.3, 1.5, (), jnp.float32)
    amplitude = centred(arg_keys[6], (SEGS, TRACERS), 1.0, 4.0, (), jnp.float32)
    pattern = centred(arg_keys[7], (TRACERS, NLON, COLS), 1.0, 5.0, ((1, 4),), jnp.float32)
    return dict(states=states, step_counts=step_counts, land=land, east_flow=east_flow, vert_mix=vert_mix, coupling=coupling, amplitude=amplitude, pattern=pattern)


MIXING = 0.1
STEP_SIZE = 0.1
EPSILON = 1e-06

def advance(field, east, west, water_here, water_east, water_west, current, current_west, pattern, vert_mix, coupling, forcing_amp, active, depth):
    open_east = water_here * water_east
    open_west = water_west * water_here
    flux_east = open_east * (jnp.maximum(current, 0.0) * field + jnp.minimum(current, 0.0) * east)
    flux_west = open_west * (jnp.maximum(current_west, 0.0) * west + jnp.minimum(current_west, 0.0) * field)
    lon_term = MIXING * (open_east * (east - field) - open_west * (field - west)) - (flux_east - flux_west)
    open_north = water_here[:, :-depth] * water_here[:, depth:]
    grad_north = open_north * (field[:, :, depth:] - field[:, :, :-depth])
    grad_north = jnp.pad(grad_north, ((0, 0), (0, 0), (depth, depth)))
    lat_term = MIXING * (grad_north[:, :, depth:] - grad_north[:, :, :-depth])
    cols = field.shape[2]
    inner = ((jnp.arange(cols - 1) + 1) % depth != 0).astype(jnp.float32)
    open_down = water_here[:, :-1] * water_here[:, 1:] * inner
    grad_down = open_down * (field[:, :, 1:] - field[:, :, :-1])
    grad_down = jnp.pad(grad_down, ((0, 0), (0, 0), (1, 1)))
    dep_term = vert_mix[:, None, None] * (grad_down[:, :, 1:] - grad_down[:, :, :-1])
    source = jnp.einsum('ts,slc->tlc', coupling, jnp.tanh(field), precision=lax.Precision.HIGHEST) + forcing_amp[:, None, None] * pattern
    fresh = water_here * (field + lon_term + lat_term + dep_term + STEP_SIZE * source)
    return jnp.where(active, fresh, field)

def reference(states, step_counts, land, east_flow, vert_mix, coupling, amplitude, pattern):
    water = land.astype(jnp.float32)
    water_east = jnp.roll(water, -1, 0)
    water_west = jnp.roll(water, 1, 0)
    current_west = jnp.roll(east_flow, 1, 0)

    def integrate(items):
        field, count, forcing_amp = items
        for section in range(STEPS):
            east = jnp.roll(field, -1, 1)
            west = jnp.roll(field, 1, 1)
            field = advance(field, east, west, water, water_east, water_west, east_flow, current_west, pattern, vert_mix, coupling, forcing_amp, section < count, DEPTH)
        return field
    ends = lax.map(integrate, (states, step_counts, amplitude))
    before = jnp.roll(ends, 1, axis=0)
    resid = water * (before - states)
    msq = lax.optimization_barrier(jnp.mean(resid * resid, axis=(2, 3)))
    scaled = resid / jnp.sqrt(msq + EPSILON)[:, :, None, None]
    mismatch = jnp.sqrt(jnp.mean(msq))
    return (scaled, mismatch)
```

```python
import functools

import jax
import jax.numpy as jnp
from jax import lax
from jax.experimental import pallas as pl
from jax.experimental.pallas import tpu as pltpu
from jax.sharding import PartitionSpec as P

STEPS = 6
SURE_STEPS = 4
DEPTH = 16
MIXING = 0.1
STEP_SIZE = 0.1
EPSILON = 1e-06
LANES = 128
F32 = jnp.float32
BF16 = jnp.bfloat16
HBM = pl.BlockSpec(memory_space=pl.ANY)
VMEM = pl.BlockSpec(memory_space=pltpu.VMEM)
SMEM = pl.BlockSpec(memory_space=pltpu.SMEM)
PARAMS = pltpu.CompilerParams(vmem_limit_bytes=48 << 20)
BOTH = ("seg", "lon")


def struct(*shape):
    return jax.ShapeDtypeStruct(shape, F32)


def iota(shape, axis):
    return lax.broadcasted_iota(jnp.int32, shape, axis)


def run_copies(pairs, sems):
    copies = [pltpu.make_async_copy(a, b, sems.at[i]) for i, (a, b) in enumerate(pairs)]
    for copy in copies:
        copy.start()
    return copies


def wait_all(copies):
    for copy in copies:
        copy.wait()


def column(row):
    count = row.shape[1]
    square = jnp.broadcast_to(row, (count, count))
    diagonal = iota((count, count), 0) == iota((count, count), 1)
    entries = jnp.sum(jnp.where(diagonal, square, 0.0), axis=1, keepdims=True)
    return jnp.broadcast_to(entries, (count, LANES))


def block_coupling(coupling, rows):
    tracers = coupling.shape[0]
    size = rows * tracers
    pick = (iota((size, tracers), 0) % tracers == iota((size, tracers), 1)).astype(BF16)
    place = (iota((tracers, size), 1) % tracers == iota((tracers, size), 0)).astype(BF16)
    tall = jnp.dot(pick, coupling.astype(BF16), preferred_element_type=F32).astype(BF16)
    full = jnp.dot(tall, place, preferred_element_type=F32)
    same = iota((size, size), 0) // tracers == iota((size, size), 1) // tracers
    return jnp.where(same, full, 0.0).astype(BF16)


def fill_coefs(water, flow, cf_ref):
    rows, cols = water.shape
    lane = iota((rows, cols), 1)
    level = lane % DEPTH
    water_east = pltpu.roll(water, rows - 1, 0)
    water_west = pltpu.roll(water, 1, 0)
    flow_west = pltpu.roll(flow, 1, 0)
    south = jnp.where(lane < DEPTH, 0.0, pltpu.roll(water, DEPTH, 1))
    north = jnp.where(lane >= cols - DEPTH, 0.0, pltpu.roll(water, cols - DEPTH, 1))
    up = jnp.where(level == 0, 0.0, pltpu.roll(water, 1, 1))
    down = jnp.where(level == DEPTH - 1, 0.0, pltpu.roll(water, cols - 1, 1))
    own = water * (
        1.0
        - MIXING * (water_east + water_west + north + south)
        - water_east * jnp.maximum(flow, 0.0)
        + water_west * jnp.minimum(flow_west, 0.0)
    )
    east = water * (MIXING - jnp.minimum(flow, 0.0))
    west = water * (MIXING + jnp.maximum(flow_west, 0.0))
    for place, value in enumerate((own, east, west, up + down, STEP_SIZE * water)):
        for row in range(rows):
            cf_ref[place, row] = jnp.broadcast_to(value[row : row + 1], (8, cols))


def masked_rows(source, first, target, at, count, cf_ref, g0):
    cols = target.shape[-1]

    def body(i, carry):
        wet = cf_ref[4, g0 + i] > 0.0
        for half in range(target.shape[1] // 8):
            part = pl.ds(8 * half, 8)
            target[at + i, part, :] = jnp.where(wet, source[first + i, part, :], 0.0)
        return carry

    lax.fori_loop(0, count, body, 0)


def copy_rows(source, first, target, at, count):
    def body(i, carry):
        target[at + i] = source[first + i]
        return carry

    lax.fori_loop(0, count, body, 0)


def one_step(source, first, target, at, count, cf_ref, g0, pattern, p0, mix, amp, kron, react_ref):
    tracers, cols = source.shape[1], source.shape[2]
    groups = cols // LANES
    size = count * tracers
    for low, high in ((0, count),) if size <= kron.shape[0] else ((0, count // 2), (count // 2, count)):
        span = (high - low) * tracers
        active = jnp.tanh(source[first + low : first + high].astype(BF16)).reshape(span, cols)
        react = jnp.dot(kron[:span, :span], active, preferred_element_type=F32)
        react_ref[low:high] = react.reshape(high - low, tracers, cols)
    lane = iota((8, LANES), 1)
    level = lane % DEPTH
    not_top = level != 0
    not_low = level != DEPTH - 1
    first_lat = lane < DEPTH
    last_lat = lane >= LANES - DEPTH

    def body(i, carry):
        for half in range(tracers // 8):
            part = slice(8 * half, 8 * half + 8)
            cells, souths, norths = [], [], []
            for group in range(groups):
                cell = source[first + i, part, LANES * group : LANES * (group + 1)]
                cells.append(cell)
                souths.append(pltpu.roll(cell, DEPTH, 1))
                norths.append(pltpu.roll(cell, LANES - DEPTH, 1))
            for group in range(groups):
                lanes = slice(LANES * group, LANES * (group + 1))
                cell = cells[group]
                south = jnp.where(first_lat, souths[group - 1] if group else 0.0, souths[group])
                north = jnp.where(last_lat, norths[group + 1] if group + 1 < groups else 0.0, norths[group])
                up = jnp.where(not_top, pltpu.roll(cell, 1, 1), 0.0)
                down = jnp.where(not_low, pltpu.roll(cell, LANES - 1, 1), 0.0)
                upright = (up + down) - cf_ref[3, g0 + i, :, lanes] * cell
                inner = (south + north) + react_ref[i, part, lanes]
                inner = inner + amp[part] * pattern[p0 + i, part, lanes] + mix[part] * upright
                fresh = cf_ref[0, g0 + i, :, lanes] * cell + cf_ref[4, g0 + i, :, lanes] * inner
                fresh = fresh + cf_ref[1, g0 + i, :, lanes] * source[first + i + 1, part, lanes]
                fresh = fresh + cf_ref[2, g0 + i, :, lanes] * source[first + i - 1, part, lanes]
                target[at + i, part, lanes] = fresh
        return carry

    lax.fori_loop(0, count, body, 0)


def gated_step(k, counted, source, first, target, at, count, *rest):
    if k < SURE_STEPS:
        one_step(source, first, target, at, count, *rest)
        return

    @pl.when(k < counted)
    def _():
        one_step(source, first, target, at, count, *rest)

    @pl.when(k >= counted)
    def _():
        copy_rows(source, first, target, at, count)


def residual(ends, first, states, count, cf_ref, g0, resid_ref, sums_ref):
    tracers, cols = ends.shape[1], ends.shape[2]

    def body(i, total):
        wet = cf_ref[4, g0 + i] > 0.0
        fresh = []
        for half in range(tracers // 8):
            part = pl.ds(8 * half, 8)
            value = ends[first + i, part, :] - jnp.where(wet, states[i, part, :], 0.0)
            resid_ref[i, part, :] = value
            square = value * value
            fresh.append(total[half] + sum(square[:, LANES * g : LANES * (g + 1)] for g in range(cols // LANES)))
        return tuple(fresh)

    zeros = tuple(jnp.zeros((8, LANES), F32) for _ in range(tracers // 8))
    totals = lax.fori_loop(0, count, body, zeros)
    for half, total in enumerate(totals):
        sums_ref[8 * half : 8 * half + 8] = total


def pack_kernel(states, pattern, land, flow, a_tail, a_head, b_tail, b_head, b_full, rows_ref, stat_ref, full_ref, sems):
    n = states.shape[2]
    tracers = states.shape[1]
    reach = STEPS
    groups = states.shape[3] // LANES
    pairs = []
    for member in range(2):
        for i in range(reach):
            pairs.append((states.at[member, :, i], rows_ref.at[2 * member, i]))
            pairs.append((states.at[member, :, n - reach + i], rows_ref.at[2 * member + 1, i]))
    for i in range(reach - 1):
        pairs.append((pattern.at[:, i], stat_ref.at[0, i]))
        pairs.append((pattern.at[:, n - reach + 1 + i], stat_ref.at[1, i]))
    loads = run_copies(pairs, sems)
    base = len(pairs)
    last = states.shape[0] - 1
    full = [
        pltpu.make_async_copy(states.at[last, t], full_ref.at[:, t], sems.at[base + t]) for t in range(tracers)
    ]
    for copy in full:
        copy.start()
    water = land[...].astype(F32)
    pad = jnp.zeros((tracers - 2 * reach, water.shape[1]), F32)
    stat_ref[0, reach - 1] = jnp.concatenate([water[:reach], flow[:reach], pad], axis=0)
    stat_ref[1, reach - 1] = jnp.concatenate([water[n - reach :], flow[n - reach :], pad], axis=0)
    wait_all(loads)
    wait_all(full)
    share = lax.rem(lax.axis_index("seg"), groups)
    lanes = pl.ds(pl.multiple_of(share * LANES, LANES), LANES)
    outs = []
    for out, side in ((a_head, 0), (a_tail, 1)):
        for g in range(groups):
            outs.append((rows_ref.at[side, :, :, pl.ds(LANES * g, LANES)], out.at[g]))
        outs.append((stat_ref.at[side, :, :, lanes], out.at[groups]))
    outs.append((rows_ref.at[2], b_head))
    outs.append((rows_ref.at[3], b_tail))
    outs.append((full_ref, b_full))
    wait_all(run_copies(outs, sems))


def inner_kernel(
    member, own_layout, start, states, pattern, land, flow, mix_row, coupling, amplitude, counts,
    save_left, save_right, resid, sums, cells, other, pat, cf, react, sems,
):
    n = land.shape[0]
    tracers = pattern.shape[0]
    reach = STEPS
    segs = counts.shape[0]
    seg_dev = states.shape[0]
    index = lax.axis_index("seg") * seg_dev + member
    index = lax.rem(index + segs, segs)
    if own_layout:
        pairs = [(start.at[member, t], cells.at[0, :, t]) for t in range(tracers)]
    else:
        pairs = [(start, cells.at[0])]
    begin = len(pairs)
    pairs += [(pattern.at[t], pat.at[:, t]) for t in range(tracers)]
    compare = (member + 1) % seg_dev
    pairs += [(states.at[compare, :, reach + i], other.at[i]) for i in range(n - 2 * reach)]
    copies = run_copies(pairs, sems)
    fill_coefs(land[...].astype(F32), flow[...], cf)
    kron = block_coupling(coupling[...], (n - 1) // 2)
    mix = column(mix_row[...]) * (1.0 / STEP_SIZE)
    amp = column(amplitude[pl.ds(index, 1), :])
    counted = counts[index]
    wait_all(copies[:begin])
    masked_rows(cells.at[0], 0, cells.at[0], 0, n, cf, 0)
    wait_all(copies[begin:])
    for k in range(STEPS):
        now, later = cells.at[k % 2], cells.at[(k + 1) % 2]
        save_left[k] = now[k : k + 2]
        save_right[k] = now[n - 2 - k : n - k]
        gated_step(
            k, counted, now, k + 1, later, k + 1, n - 2 - 2 * k, cf, k + 1, pat, k + 1, mix, amp, kron, react
        )
    residual(cells.at[STEPS % 2], reach, other, n - 2 * reach, cf, reach, resid, sums)


def edge_kernel(
    member, left, halo, saved, statics, states, pattern, land, flow, mix_row, coupling, amplitude, counts, *rest,
):
    given, (resid, sums, cells, other, pat, cf, react, water, current, sems) = rest[:-10], rest[-10:]
    n = land.shape[0]
    tracers = pattern.shape[0]
    cols = land.shape[1]
    reach = STEPS
    segs = counts.shape[0]
    seg_dev = states.shape[0]
    index = lax.rem(lax.axis_index("seg") * seg_dev + member + segs, segs)
    own = 0 if left else n - reach
    compare = (member + 1) % seg_dev
    pairs = [(states.at[compare, :, own + i], other.at[i]) for i in range(reach)]
    low = 0 if left else n - 8
    h0, w0 = (0, reach) if left else (8, 0)
    pairs += [(pattern.at[:, own + i], pat.at[(reach if left else 2) + i]) for i in range(reach)]
    p0 = 1 if left else 8
    pairs += [(statics.at[i], pat.at[p0 + i]) for i in range(reach - 1)]
    begin = cells.at[0, 0:reach] if left else cells.at[0, 2 : 2 + reach]
    if len(halo.shape) == 4:
        for g in range(cols // LANES):
            pairs.append((halo.at[g], begin.at[:, :, pl.ds(LANES * g, LANES)]))
    else:
        pairs.append((halo, begin))
    copies = run_copies(pairs, sems)
    edge = pltpu.make_async_copy(statics.at[reach - 1], react.at[0], sems.at[len(pairs)])
    edge.start()
    edge.wait()
    water[...] = jnp.zeros_like(water)
    current[...] = jnp.zeros_like(current)
    water[h0 : h0 + reach] = react[0, 0:reach]
    current[h0 : h0 + reach] = react[0, reach : 2 * reach]
    water[w0 : w0 + 8] = land[low : low + 8].astype(F32)
    current[w0 : w0 + 8] = flow[low : low + 8]
    fill_coefs(water[...], current[...], cf)
    kron = block_coupling(coupling[...], reach)
    mix = column(mix_row[...]) * (1.0 / STEP_SIZE)
    amp = column(amplitude[pl.ds(index, 1), :])
    counted = counts[index]
    wait_all(copies)
    place = 0 if left else 2
    masked_rows(cells.at[0], place, cells.at[0], place, reach, cf, h0)
    for k in range(STEPS):
        now, later = cells.at[k % 2], cells.at[(k + 1) % 2]
        now[reach if left else 0 : (reach if left else 0) + 2] = saved[k]
        g0 = (k if left else STEPS - k) + 1
        gated_step(k, counted, now, 1, later, place, reach, cf, g0, pat, g0, mix, amp, kron, react)
    residual(cells.at[STEPS % 2], place, other, reach, cf, reach if left else 2, resid, sums)
    if given:
        sums_a, sums_b, share = given[:3], given[3:5], given[5]
        first = sums_b[0][...] + sums_b[1][...] + sums[...]
        second = sums_a[0][...] + sums_a[1][...] + sums_a[2][...]
        line = jnp.zeros((1, LANES), F32)
        for at, total in enumerate((first, second)):
            whole = jnp.sum(total, axis=1, keepdims=True)
            spot = iota((tracers, LANES), 1) == iota((tracers, LANES), 0) + tracers * at
            line = line + jnp.sum(jnp.where(spot, whole, 0.0), axis=0, keepdims=True)
        share[...] = jnp.broadcast_to(line, share.shape)


def merge_kernel(first, second, *rest):
    others, (left, right, sems) = rest[:-3], rest[-3:]
    groups = left.shape[2] // LANES
    pair = lax.rem(lax.axis_index("seg"), groups) // 2
    pairs = []
    for shift, block in enumerate([None, *others]):
        source = lax.rem(pair - shift + groups, groups // 2) if shift else pair
        for core in range(2):
            part = (first, second)[core] if block is None else block.at[core]
            lanes = pl.ds(pl.multiple_of((2 * source + core) * LANES, LANES), LANES)
            pairs.append((part.at[0], left.at[:, :, lanes]))
            pairs.append((part.at[1], right.at[:, :, lanes]))
    wait_all(run_copies(pairs, sems))


def scale_kernel(gathered, b_left, b_inner, b_right, a_left, a_inner, a_right, out, mismatch, work, sems):
    n = out.shape[2]
    tracers, cols = out.shape[1], out.shape[3]
    all_rows = gathered.shape[0]
    lon = lax.axis_size("lon")
    mine = lax.axis_index("seg")
    row = iota((all_rows, LANES), 0)
    values = gathered[...]
    here = jnp.sum(jnp.where(row // lon == mine, values, 0.0), axis=0, keepdims=True)
    cells = float(n * lon * cols)
    year = jnp.sum(jnp.sum(values, axis=0, keepdims=True), axis=1, keepdims=True)
    segs = all_rows // lon * out.shape[0]
    mismatch[...] = jnp.sqrt(year / (cells * segs * tracers))
    copies = []
    for member, parts in enumerate(((b_left, b_inner, b_right), (a_left, a_inner, a_right))):
        spot = iota((tracers, LANES), 1) == iota((tracers, LANES), 0) + tracers * member
        total = jnp.sum(jnp.where(spot, jnp.broadcast_to(here, (tracers, LANES)), 0.0), axis=1, keepdims=True)
        factor = jnp.broadcast_to(1.0 / jnp.sqrt(total / cells + EPSILON), (tracers, cols))
        at = 0
        for part in parts:
            for i in range(part.shape[0]):
                work[member, at] = part[i] * factor
                copy = pltpu.make_async_copy(work.at[member, at], out.at[member, :, at], sems.at[member * n + at])
                copy.start()
                copies.append(copy)
                at += 1
    wait_all(copies)


def moved(value, ds, dl):
    seg, lon = lax.axis_size("seg"), lax.axis_size("lon")
    pairs = [(s * lon + l, (s + ds) % seg * lon + (l + dl) % lon) for s in range(seg) for l in range(lon)]
    return lax.ppermute(value, BOTH, pairs)


def shards(states, step_counts, land, east_flow, vert_mix, coupling, amplitude, pattern):
    seg_dev, tracers, n, cols = states.shape
    reach = STEPS
    seg = lax.axis_size("seg")
    groups = cols // LANES
    mix_row = vert_mix.reshape(1, tracers)
    dma = lambda count: pltpu.SemaphoreType.DMA((count,))

    a_tail, a_head, b_tail, b_head, b_full = pl.pallas_call(
        pack_kernel,
        in_specs=[HBM, HBM, VMEM, VMEM],
        out_specs=[HBM] * 5,
        out_shape=[struct(groups + 1, reach, tracers, LANES)] * 2 + [struct(reach, tracers, cols)] * 2
        + [struct(n, tracers, cols)],
        scratch_shapes=[
            pltpu.VMEM((4, reach, tracers, cols), F32),
            pltpu.VMEM((2, reach, tracers, cols), F32),
            pltpu.VMEM((n, tracers, cols), F32),
            dma(4 * reach + 2 * reach + tracers),
        ],
        compiler_params=PARAMS,
    )(states, pattern, land, east_flow)
    with jax.named_scope("exchange"):
        a_left = moved(a_tail, 0, 1)
        a_right = moved(a_head, 0, -1)
        b_start = moved(b_full, 1, 0)
        b_left = moved(b_tail, 1, 1)
        b_right = moved(b_head, 1, -1)

    flops = 40 * n * tracers * cols * STEPS

    def inner(member, start):
        rows = n - 2 * reach
        return pl.pallas_call(
            functools.partial(inner_kernel, member, member >= 0),
            in_specs=[HBM, HBM, HBM, VMEM, VMEM, VMEM, VMEM, VMEM, SMEM],
            out_specs=[VMEM] * 4,
            out_shape=[struct(STEPS, 2, tracers, cols)] * 2 + [struct(rows, tracers, cols), struct(tracers, LANES)],
            scratch_shapes=[
                pltpu.VMEM((2, n, tracers, cols), F32),
                pltpu.VMEM((rows, tracers, cols), F32),
                pltpu.VMEM((n, tracers, cols), F32),
                pltpu.VMEM((5, n, 8, cols), F32),
                pltpu.VMEM((n, tracers, cols), F32),
                dma(2 * tracers + rows),
            ],
            compiler_params=PARAMS,
            cost_estimate=pl.CostEstimate(flops=flops, bytes_accessed=8 << 20, transcendentals=0),
        )(start, states, pattern, land, east_flow, mix_row, coupling, amplitude, step_counts)

    a_save_left, a_save_right, a_inner, a_sums = inner(0, states)

    with jax.named_scope("statics"):
        mine = jnp.stack([a_left[groups], a_right[groups]])
        span = min(groups, seg)
        other = lax.ppermute(mine, "seg", [(i, i ^ 1) for i in range(seg)])
        odd = lax.axis_index("seg") % 2
        first = jnp.where(odd == 0, mine, other)
        second = jnp.where(odd == 0, other, mine)
        pair = jnp.stack([first, second])
        blocks = [
            lax.ppermute(pair, "seg", [(i, i // span * span + (i + 2 * s) % span) for i in range(seg)])
            for s in range(1, span // 2)
        ]
        stat_left, stat_right = pl.pallas_call(
            merge_kernel,
            in_specs=[HBM] * (2 + len(blocks)),
            out_specs=[HBM] * 2,
            out_shape=[struct(reach, tracers, cols)] * 2,
            scratch_shapes=[dma(2 * span)],
            compiler_params=PARAMS,
        )(first, second, *blocks)

    b_save_left, b_save_right, b_inner, b_sums = inner(-1, b_start)

    def edge(member, left, halo, saved, statics, given=()):
        outs = [struct(reach, tracers, cols), struct(tracers, LANES)]
        if given:
            outs = outs + [struct(seg * lax.axis_size("lon"), LANES)]
        window = 16
        return pl.pallas_call(
            functools.partial(edge_call, member, left, len(given)),
            in_specs=[HBM, VMEM, HBM, HBM, HBM, VMEM, VMEM, VMEM, VMEM, VMEM, SMEM] + [VMEM] * len(given),
            out_specs=[VMEM] * len(outs),
            out_shape=outs,
            scratch_shapes=[
                pltpu.VMEM((2, reach + 2, tracers, cols), F32),
                pltpu.VMEM((reach, tracers, cols), F32),
                pltpu.VMEM((window, tracers, cols), F32),
                pltpu.VMEM((5, window, 8, cols), F32),
                pltpu.VMEM((reach, tracers, cols), F32),
                pltpu.VMEM((window, cols), F32),
                pltpu.VMEM((window, cols), F32),
                dma(3 * reach + groups + 2),
            ],
            compiler_params=PARAMS,
            cost_estimate=pl.CostEstimate(flops=flops // 4, bytes_accessed=3 << 20, transcendentals=0),
        )(halo, saved, statics, states, pattern, land, east_flow, mix_row, coupling, amplitude, step_counts, *given)

    al_resid, al_sums = edge(0, True, a_left, a_save_left, stat_left)
    ar_resid, ar_sums = edge(0, False, a_right, a_save_right, stat_right)
    bl_resid, bl_sums = edge(-1, True, b_left, b_save_left, stat_left)
    br_resid, _, share = edge(
        -1, False, b_right, b_save_right, stat_right, (a_sums, al_sums, ar_sums, b_sums, bl_sums)
    )
    with jax.named_scope("mean_squares"):
        gathered = lax.all_to_all(share, BOTH, 0, 0, tiled=True)
    scaled, mismatch = pl.pallas_call(
        scale_kernel,
        in_specs=[VMEM] * 7,
        out_specs=[HBM, VMEM],
        out_shape=[struct(seg_dev, tracers, n, cols), struct(1, 1)],
        scratch_shapes=[pltpu.VMEM((seg_dev, n, tracers, cols), F32), dma(seg_dev * n)],
        compiler_params=PARAMS,
    )(gathered, bl_resid, b_inner, br_resid, al_resid, a_inner, ar_resid)
    return (scaled, mismatch.reshape(()))


def edge_call(member, left, given, *refs):
    inputs, rest = refs[:11], refs[11:]
    extra, rest = rest[:given], rest[given:]
    outs, scratch = rest[: 3 if given else 2], rest[3 if given else 2 :]
    edge_kernel(member, left, *inputs, *extra, *outs[2:], *outs[:2], *scratch)


def solution(mesh):
    in_specs = (
        P("seg", None, "lon", None),
        P(),
        P("lon", None),
        P("lon", None),
        P(),
        P(),
        P(),
        P(None, "lon", None),
    )
    out_specs = (P("seg", None, "lon", None), P())
    return jax.shard_map(shards, mesh=mesh, in_specs=in_specs, out_specs=out_specs, check_vma=False)
```

```python
import functools

import jax
import jax.numpy as jnp
from jax import lax
from jax.experimental import pallas as pl
from jax.experimental.pallas import tpu as pltpu
from jax.sharding import PartitionSpec as P

STEPS = 6
SURE_STEPS = 4
DEPTH = 16
MIXING = 0.1
STEP_SIZE = 0.1
EPSILON = 1e-06
LANES = 128
WINDOW = 16
OWN = 8
MOST_ROWS = 12
PLACES = 16
F32 = jnp.float32
BF16 = jnp.bfloat16
ANY = pl.BlockSpec(memory_space=pl.ANY)
VMEM = pl.BlockSpec(memory_space=pltpu.VMEM)
SMEM = pl.BlockSpec(memory_space=pltpu.SMEM)
BOTH = ("seg", "lon")


def call(kernel, inputs, in_specs, out_specs, out_shape, scratch, room=30):
    return pl.pallas_call(
        kernel,
        in_specs=in_specs,
        out_specs=out_specs,
        out_shape=out_shape,
        scratch_shapes=scratch,
        compiler_params=pltpu.CompilerParams(vmem_limit_bytes=room << 20),
        cost_estimate=pl.CostEstimate(flops=1, bytes_accessed=1, transcendentals=0),
    )(*inputs)


def struct(*shape, dtype=F32):
    return jax.ShapeDtypeStruct(shape, dtype)


def buffer(*shape, dtype=F32):
    return pltpu.VMEM(shape, dtype)


def semaphores(count):
    return pltpu.SemaphoreType.DMA((count,))


def iota(shape, axis):
    return lax.broadcasted_iota(jnp.int32, shape, axis)


def run_copies(pairs, sems):
    copies = [pltpu.make_async_copy(a, b, sems.at[i]) for i, (a, b) in enumerate(pairs)]
    for copy in copies:
        copy.start()
    return copies


def wait_all(copies):
    for copy in copies:
        copy.wait()


def column(row):
    count = row.shape[1]
    square = jnp.broadcast_to(row, (count, count))
    diagonal = iota((count, count), 0) == iota((count, count), 1)
    entries = jnp.sum(jnp.where(diagonal, square, 0.0), axis=1, keepdims=True)
    return jnp.broadcast_to(entries, (count, LANES))


def block_coupling(coupling, rows):
    tracers = coupling.shape[0]
    size = rows * tracers
    pick = (iota((size, tracers), 0) % tracers == iota((size, tracers), 1)).astype(BF16)
    place = (iota((tracers, size), 1) % tracers == iota((tracers, size), 0)).astype(BF16)
    tall = jnp.dot(pick, coupling.astype(BF16), preferred_element_type=F32).astype(BF16)
    full = jnp.dot(tall, place, preferred_element_type=F32)
    same = iota((size, size), 0) // tracers == iota((size, size), 1) // tracers
    return jnp.where(same, full, 0.0).astype(BF16)


def neighbour_matrix():
    row, col = iota((4 * LANES, 2 * LANES), 0), iota((4 * LANES, 2 * LANES), 1)
    source, corner = row % LANES, row >= 2 * LANES
    lane, lat = col % LANES, col >= LANES
    level = lane % DEPTH
    up = (source == lane - 1) & (level != 0)
    down = (source == lane + 1) & (level != DEPTH - 1)
    vertical = jnp.logical_not(lat) & jnp.logical_not(corner) & (up | down)
    beside = (source == lane - DEPTH) | (source == lane + DEPTH)
    across = (source == lane - DEPTH + LANES) | (source == lane + DEPTH - LANES)
    near = lat & ((beside & jnp.logical_not(corner)) | (across & corner))
    return jnp.where(vertical | near, 1.0, 0.0).astype(BF16)


def fill_coefs(water, flow, mix, cf_ref, own_ref):
    rows, cols = water.shape
    tracers = mix.shape[0]
    lane = iota((rows, cols), 1)
    level = lane % DEPTH
    water_east = pltpu.roll(water, rows - 1, 0)
    water_west = pltpu.roll(water, 1, 0)
    flow_west = pltpu.roll(flow, 1, 0)
    south = jnp.where(lane < DEPTH, 0.0, pltpu.roll(water, DEPTH, 1))
    north = jnp.where(lane >= cols - DEPTH, 0.0, pltpu.roll(water, cols - DEPTH, 1))
    up = jnp.where(level == 0, 0.0, pltpu.roll(water, 1, 1))
    down = jnp.where(level == DEPTH - 1, 0.0, pltpu.roll(water, cols - 1, 1))
    own = water * (
        1.0
        - MIXING * (water_east + water_west + north + south)
        - water_east * jnp.maximum(flow, 0.0)
        + water_west * jnp.minimum(flow_west, 0.0)
    )
    east = water * (MIXING - jnp.minimum(flow, 0.0))
    west = water * (MIXING + jnp.maximum(flow_west, 0.0))
    faces = water * (up + down)
    mixes = jnp.concatenate([mix] * (cols // LANES), axis=1)
    for row in range(rows):
        for place, value in enumerate((east, west, STEP_SIZE * water)):
            cf_ref[place, row] = jnp.broadcast_to(value[row : row + 1], (8, cols))
        here = jnp.broadcast_to(own[row : row + 1], (tracers, cols))
        own_ref[row] = here - mixes * jnp.broadcast_to(faces[row : row + 1], (tracers, cols))


def masked_rows(source, first, target, at, count, cf_ref, g0):
    def body(i, carry):
        wet = cf_ref[2, g0 + i] > 0.0
        for half in range(target.shape[1] // 8):
            part = slice(8 * half, 8 * half + 8)
            target[at + i, part, :] = jnp.where(wet, source[first + i, part, :], 0.0)
        return carry

    lax.fori_loop(0, count, body, 0, unroll=2)


def one_step(rows, mix, kron, near, tanh_ref, lhs_ref):
    tracers, cols = rows[0][0].shape[1], rows[0][0].shape[2]
    groups = cols // LANES
    left_half = iota((tracers, LANES), 1) < LANES // 2
    nothing = jnp.zeros((tracers, LANES), BF16)
    for i, (source, at, *_) in enumerate(rows):
        highs, lows = [], []
        for g in range(groups):
            lanes = slice(LANES * g, LANES * (g + 1))
            cell = source[at, :, lanes]
            high = cell.astype(BF16)
            low = (cell - high.astype(F32)).astype(BF16)
            tanh_ref[i, :, lanes] = jnp.tanh(high)
            lhs_ref[g, i, :, 0:LANES] = high
            lhs_ref[g, i, :, LANES : 2 * LANES] = low
            highs.append(high)
            lows.append(low)
        for g in range(groups):
            for place, values in ((2, highs), (3, lows)):
                after = values[g + 1] if g + 1 < groups else nothing
                before = values[g - 1] if g else nothing
                lhs_ref[g, i, :, place * LANES : (place + 1) * LANES] = jnp.where(left_half, after, before)
    count = len(rows)
    span = count * tracers
    deep = -(-span // LANES) * LANES

    def sides_of(first, last):
        lhs = lhs_ref[first:last, 0:count].reshape((last - first) * span, 4 * LANES)
        return jnp.dot(lhs, near[...], preferred_element_type=F32)

    def react_of(g):
        active = tanh_ref[0 : deep // tracers, :, LANES * g : LANES * (g + 2)].reshape(deep, 2 * LANES)
        return jnp.dot(kron[:span, :deep], active, preferred_element_type=F32)

    whole = sides_of(0, groups) if count <= 8 else None
    sides = sides_of(0, 1) if whole is None else None
    react = react_of(0)
    for g in range(groups):
        lanes = slice(LANES * g, LANES * (g + 1))
        if whole is None:
            after = sides_of(g + 1, g + 2) if g + 1 < groups else None
        else:
            sides = whole[g * span : (g + 1) * span]
        later = react_of(g + 1) if g % 2 and g + 1 < groups else react
        reacted = react[:, LANES * (g % 2) : LANES * (g % 2 + 1)]
        for half in range(tracers // 8):
            part = slice(8 * half, 8 * half + 8)
            for i, (source, at, target, to, cf_ref, own_ref, force, p) in enumerate(rows):
                base = tracers * i + 8 * half
                inner = sides[base : base + 8, LANES:] + reacted[base : base + 8]
                inner = inner + force[p, part, lanes] + mix[part] * sides[base : base + 8, :LANES]
                fresh = own_ref[p, part, lanes] * source[at, part, lanes] + cf_ref[2, p, :, lanes] * inner
                fresh = fresh + cf_ref[0, p, :, lanes] * source[at + 1, part, lanes]
                fresh = fresh + cf_ref[1, p, :, lanes] * source[at - 1, part, lanes]
                target[to, part, lanes] = fresh
        react = later
        if whole is None:
            sides = after


def gated_step(k, counted, rows, *rest):
    parts = -(-len(rows) // MOST_ROWS)
    size = -(-len(rows) // parts)

    def work():
        for low in range(0, len(rows), size):
            one_step(rows[low : low + size], *rest)

    if k < SURE_STEPS:
        work()
        return
    pl.when(k < counted)(work)

    @pl.when(k >= counted)
    def _():
        for source, at, target, to, *_ in rows:
            target[to] = source[at]


def residual(ends, first, states, count, cf_ref, g0, resid_ref, r0):
    tracers, cols = ends.shape[1], ends.shape[2]

    def body(i, total):
        wet = cf_ref[2, g0 + i] > 0.0
        fresh = []
        for half in range(tracers // 8):
            part = slice(8 * half, 8 * half + 8)
            value = ends[first + i, part, :] - jnp.where(wet, states[i, part, :], 0.0)
            resid_ref[r0 + i, part, :] = value
            square = value * value
            fresh.append(total[half] + sum(square[:, LANES * g : LANES * (g + 1)] for g in range(cols // LANES)))
        return tuple(fresh)

    zeros = tuple(jnp.zeros((8, LANES), F32) for _ in range(tracers // 8))
    return jnp.concatenate(lax.fori_loop(0, count, body, zeros, unroll=2), axis=0)


def seg_index(member, counts, seg_dev):
    segs = counts.shape[0]
    return lax.rem(lax.axis_index("seg") * seg_dev + member + segs, segs)


def pack_first_kernel(states, pattern, land, flow, stat_tail, stat_head, tail, head, stat_ref, sems):
    n, cols = land.shape
    tracers = pattern.shape[0]
    reach = STEPS
    part = cols // 2
    share = lax.rem(lax.axis_index("seg"), 2)
    mine = pl.ds(pl.multiple_of(share * part, LANES), part)
    pairs = []
    for i in range(reach):
        pairs.append((states.at[0, :, i], head.at[i]))
        pairs.append((states.at[0, :, n - reach + i], tail.at[i]))
    for i in range(reach - 1):
        pairs.append((pattern.at[:, i, mine], stat_head.at[i]))
        pairs.append((pattern.at[:, n - reach + 1 + i, mine], stat_tail.at[i]))
    copies = run_copies(pairs, sems)
    water = land[...].astype(F32)
    pad = jnp.zeros((tracers - 2 * reach, cols), F32)
    stat_ref[0] = jnp.concatenate([water[:reach], flow[:reach], pad], axis=0)
    stat_ref[1] = jnp.concatenate([water[n - reach :], flow[n - reach :], pad], axis=0)
    for side, out in ((0, stat_head), (1, stat_tail)):
        copy = pltpu.make_async_copy(
            stat_ref.at[side, :, mine], out.at[reach - 1], sems.at[len(copies)]
        )
        copy.start()
        copies.append(copy)
    wait_all(copies)


def pack_last_kernel(states, after, tail, head, full, sems):
    n, last = states.shape[2], states.shape[0] - 1
    pairs = [(states.at[last], full)]
    for i in range(STEPS):
        pairs.append((states.at[last, :, i], head.at[i]))
        pairs.append((states.at[last, :, n - STEPS + i], tail.at[i]))
    wait_all(run_copies(pairs, sems))


def inner_kernel(
    member, shared, start, states, pattern, land, flow, mix_row, coupling, amplitude, counts, *rest,
):
    given, rest = (rest[:5], rest[5:]) if shared else (rest[:1], rest[1:])
    save_left, save_right, resid, sums = rest[:4]
    cells, other, force, tanh_ref, lhs_ref, sems = rest[-6:]
    kron, near, own, cf = given[:4] if shared else rest[4:8]
    n = land.shape[0]
    tracers = pattern.shape[0]
    reach = STEPS
    seg_dev = states.shape[0]
    index = seg_index(member, counts, seg_dev)
    begin = start.at[member] if len(start.shape) == 4 else start
    pairs = [(begin.at[t], cells.at[0, :, t]) for t in range(tracers)]
    first = len(pairs)
    pairs += [(pattern.at[t], force.at[:, t]) for t in range(tracers)]
    compare = (member + 1) % seg_dev
    pairs += [(states.at[compare, :, reach + i], other.at[i]) for i in range(n - 2 * reach)]
    copies = run_copies(pairs, sems)
    mix = column(mix_row[...])
    if not shared:
        fill_coefs(land[...].astype(F32), flow[...], mix, cf, own)
        kron[...] = block_coupling(coupling[...], PLACES)
        near[...] = neighbour_matrix()
    amp = column(amplitude[pl.ds(index, 1), :])
    counted = counts[index]
    tanh_ref[...] = jnp.zeros_like(tanh_ref)
    wait_all(copies[:first])
    masked_rows(cells.at[0], 0, cells.at[0], 0, n, cf, 0)
    wait_all(copies[first:])
    forced(force, amp, n)
    mix = mix * (1.0 / STEP_SIZE)
    for k in range(STEPS):
        now, later = cells.at[k % 2], cells.at[(k + 1) % 2]
        save_left[k] = now[k : k + 2]
        save_right[k] = now[n - 2 - k : n - k]
        rows = [(now, r, later, r, cf, own, force, r) for r in range(k + 1, n - 1 - k)]
        gated_step(k, counted, rows, mix, kron, near, tanh_ref, lhs_ref)
    sums[...] = residual(cells.at[STEPS % 2], reach, other, n - 2 * reach, cf, reach, resid, 0)


def forced(force, amp, rows):
    groups = force.shape[2] // LANES
    wide = jnp.concatenate([amp] * groups, axis=1)

    def body(i, carry):
        force[i] = force[i] * wide
        return carry

    lax.fori_loop(0, rows, body, 0, unroll=2)


def edge_kernel(member, sides, last, *refs):
    per_side = 5
    count = len(sides)
    inputs = [refs[per_side * s : per_side * (s + 1)] for s in range(count)]
    refs = refs[per_side * count :]
    states, mix_row, amplitude, counts, kron, near, after = refs[:7]
    given, refs = (refs[7:11], refs[11:]) if last else ((), refs[7:])
    resid, sums = refs[0], refs[1]
    cells, other, force, tanh_ref, lhs_ref, sems = refs[-6:]
    n = states.shape[2]
    cols, tracers = states.shape[3], states.shape[1]
    reach = STEPS
    seg_dev = states.shape[0]
    index = seg_index(member, counts, seg_dev)
    compare = (member + 1) % seg_dev
    pairs = []
    for s, left in enumerate(sides):
        halo, _, _, _, pat = inputs[s]
        place = 0 if left else 2
        pairs.append((halo, cells.at[s, 0, place : place + reach]))
        pairs += [(states.at[compare, :, (0 if left else n - reach) + i], other.at[s, i]) for i in range(reach)]
    copies = run_copies(pairs, sems)
    mix = column(mix_row[...]) * (1.0 / STEP_SIZE)
    amp = column(amplitude[pl.ds(index, 1), :])
    wide = jnp.concatenate([amp] * (cols // LANES), axis=1)
    counted = counts[index]
    for s in range(count):
        pat = inputs[s][4]

        def body(i, carry, s=s, pat=pat):
            force[s, i] = pat[i] * wide
            return carry

        lax.fori_loop(1, 13, body, 0, unroll=2)
    tanh_ref[...] = jnp.zeros_like(tanh_ref)
    wait_all(copies)
    for s, left in enumerate(sides):
        place = 0 if left else 2
        masked_rows(cells.at[s, 0], place, cells.at[s, 0], place, reach, inputs[s][2], 0 if left else OWN)
    for k in range(STEPS):
        rows = []
        for s, left in enumerate(sides):
            _, saved, cf, own, _ = inputs[s]
            now, later = cells.at[s, k % 2], cells.at[s, (k + 1) % 2]
            free = reach if left else 0
            now[free : free + 2] = saved[k]
            g0 = (k if left else STEPS - k) + 1
            place = 0 if left else 2
            rows += [(now, 1 + i, later, place + i, cf, own, force.at[s], g0 + i) for i in range(reach)]
        gated_step(k, counted, rows, mix, kron, near, tanh_ref, lhs_ref)
    total = 0.0
    for s, left in enumerate(sides):
        place = 0 if left else 2
        ends = cells.at[s, STEPS % 2]
        total = total + residual(
            ends, place, other.at[s], reach, inputs[s][2], reach if left else 2, resid, reach * s
        )
    sums[...] = total
    if last:
        share = refs[2]
        first = given[0][...] + given[1][...] + total
        second = given[2][...] + given[3][...]
        line = jnp.zeros((1, LANES), F32)
        for at, part in enumerate((first, second)):
            whole = jnp.sum(part, axis=1, keepdims=True)
            spot = iota((tracers, LANES), 1) == iota((tracers, LANES), 0) + tracers * at
            line = line + jnp.sum(jnp.where(spot, whole, 0.0), axis=0, keepdims=True)
        share[...] = jnp.broadcast_to(line, share.shape)


def merge_kernel(blocks, *refs):
    shares, refs = refs[:blocks], refs[blocks:]
    pattern, land, flow, mix_row, after = refs[:5]
    outs, (stat, water, current, sems) = refs[5:11], refs[11:]
    n, cols = land.shape
    reach = STEPS
    part = cols // 2
    core = lax.rem(lax.axis_index("seg"), 2)
    pairs = []
    for block, which in zip(shares, (core, 1 - core)):
        lanes = pl.ds(pl.multiple_of(which * part, LANES), part)
        for side in range(2):
            pairs.append((block.at[side, reach - 1], stat.at[side, :, lanes]))
            p0 = OWN if side else 1
            pairs.append(
                (block.at[side, pl.ds(0, reach - 1)], outs[3 * side + 2].at[pl.ds(p0, reach - 1), :, lanes])
            )
    for i in range(reach):
        pairs.append((pattern.at[:, i], outs[2].at[reach + i]))
        pairs.append((pattern.at[:, n - reach + i], outs[5].at[2 + i]))
    copies = run_copies(pairs, sems)
    mix = column(mix_row[...])
    wait_all(copies)
    for side in range(2):
        low, h0, w0 = (n - OWN, OWN, 0) if side else (0, 0, reach)
        water[...] = jnp.zeros_like(water)
        current[...] = jnp.zeros_like(current)
        water[h0 : h0 + reach] = stat[side, 0:reach]
        current[h0 : h0 + reach] = stat[side, reach : 2 * reach]
        water[w0 : w0 + OWN] = land[low : low + OWN].astype(F32)
        current[w0 : w0 + OWN] = flow[low : low + OWN]
        fill_coefs(water[...], current[...], mix, outs[3 * side], outs[3 * side + 1])


def scale_kernel(gathered, b_left, b_inner, b_right, a_edges, a_inner, out, mismatch, work, sems):
    n = out.shape[2]
    tracers, cols = out.shape[1], out.shape[3]
    all_rows = gathered.shape[0]
    lon = lax.axis_size("lon")
    mine = lax.axis_index("seg")
    row = iota((all_rows, LANES), 0)
    values = gathered[...]
    here = jnp.sum(jnp.where(row // lon == mine, values, 0.0), axis=0, keepdims=True)
    cells = float(n * lon * cols)
    year = jnp.sum(jnp.sum(values, axis=0, keepdims=True), axis=1, keepdims=True)
    segs = all_rows // lon * out.shape[0]
    mismatch[...] = jnp.sqrt(year / (cells * segs * tracers))
    reach = STEPS
    b_parts = ((b_left, 0, reach), (b_inner, 0, n - 2 * reach), (b_right, 0, reach))
    a_parts = ((a_edges, 0, reach), (a_inner, 0, n - 2 * reach), (a_edges, reach, reach))
    copies = []
    for member, parts in enumerate((b_parts, a_parts)):
        spot = iota((tracers, LANES), 1) == iota((tracers, LANES), 0) + tracers * member
        total = jnp.sum(jnp.where(spot, jnp.broadcast_to(here, (tracers, LANES)), 0.0), axis=1, keepdims=True)
        factor = jnp.broadcast_to(1.0 / jnp.sqrt(total / cells + EPSILON), (tracers, cols))
        at = 0
        for part, first, count in parts:
            for i in range(count):
                work[member, at] = part[first + i] * factor
                copy = pltpu.make_async_copy(work.at[member, at], out.at[member, :, at], sems.at[member * n + at])
                copy.start()
                copies.append(copy)
                at += 1
    wait_all(copies)


def moved(value, ds, dl):
    seg, lon = lax.axis_size("seg"), lax.axis_size("lon")
    pairs = [(s * lon + l, (s + ds) % seg * lon + (l + dl) % lon) for s in range(seg) for l in range(lon)]
    return lax.ppermute(value, BOTH, pairs)


def shards(states, step_counts, land, east_flow, vert_mix, coupling, amplitude, pattern):
    seg_dev, tracers, n, cols = states.shape
    reach = STEPS
    seg = lax.axis_size("seg")
    groups = cols // LANES
    mix_row = vert_mix.reshape(1, tracers)

    s_tail, s_head, a_tail, a_head = call(
        pack_first_kernel,
        (states, pattern, land, east_flow),
        [ANY, ANY, VMEM, VMEM],
        [VMEM] * 4,
        [struct(reach, tracers, cols // 2)] * 2 + [struct(reach, tracers, cols)] * 2,
        [buffer(2, tracers, cols), semaphores(4 * reach)],
        room=62,
    )
    b_tail, b_head, b_full = call(
        pack_last_kernel,
        (states, a_tail),
        [ANY, ANY],
        [VMEM] * 3,
        [struct(reach, tracers, cols)] * 2 + [struct(tracers, n, cols)],
        [semaphores(2 * reach + 1)],
        room=62,
    )
    with jax.named_scope("exchange"):
        s_left = moved(s_tail, 0, 1)
        s_right = moved(s_head, 0, -1)
        a_left = moved(a_tail, 0, 1)
        a_right = moved(a_head, 0, -1)
        b_start = moved(b_full, 1, 0)
        b_left = moved(b_tail, 1, 1)
        b_right = moved(b_head, 1, -1)

    def inner(member, start, given):
        rows = n - 2 * reach
        size = PLACES * tracers
        outs = [struct(STEPS, 2, tracers, cols)] * 2 + [struct(rows, tracers, cols), struct(tracers, LANES)]
        if len(given) == 1:
            outs = outs + [struct(size, size, dtype=BF16), struct(4 * LANES, 2 * LANES, dtype=BF16)]
            outs = outs + [struct(n, tracers, cols), struct(3, n, 8, cols)]
        return call(
            functools.partial(inner_kernel, member, len(given) > 1),
            (start, states, pattern, land, east_flow, mix_row, coupling, amplitude, step_counts, *given),
            [ANY, ANY, ANY, VMEM, VMEM, VMEM, VMEM, VMEM, SMEM] + [VMEM, VMEM, VMEM, VMEM, ANY][-len(given) :],
            [VMEM] * len(outs),
            outs,
            [
                buffer(2, n, tracers, cols),
                buffer(rows, tracers, cols),
                buffer(n, tracers, cols),
                buffer(PLACES, tracers, cols, dtype=BF16),
                buffer(groups, MOST_ROWS, tracers, 4 * LANES, dtype=BF16),
                semaphores(2 * tracers + rows),
            ],
        )

    a_save_left, a_save_right, a_inner, a_sums, kron, near, own, cf = inner(0, states, (b_tail,))

    with jax.named_scope("statics"):
        s_left, s_right, a_sums = lax.optimization_barrier((s_left, s_right, a_sums))
        mine = jnp.stack([s_left, s_right])
        other = lax.ppermute(mine, "seg", [(i, i ^ 1) for i in range(seg)])
        blocks = [mine, other]
    b_save_left, b_save_right, b_inner, b_sums = inner(-1, b_start, (kron, near, own, cf, a_sums))
    left_cf, left_own, left_pat, right_cf, right_own, right_pat = call(
        functools.partial(merge_kernel, len(blocks)),
        (*blocks, pattern, land, east_flow, mix_row, b_sums),
        [ANY] * len(blocks) + [ANY, VMEM, VMEM, VMEM, ANY],
        [VMEM] * 6,
        [struct(3, WINDOW, 8, cols), struct(WINDOW, tracers, cols), struct(WINDOW, tracers, cols)] * 2,
        [
            buffer(2, tracers, cols),
            buffer(WINDOW, cols),
            buffer(WINDOW, cols),
            semaphores(8 * len(blocks) + 2 * reach),
        ],
    )
    left_statics, right_statics = (left_cf, left_own, left_pat), (right_cf, right_own, right_pat)

    def edge(member, sides, parts, after, given=()):
        outs = [struct(reach * len(sides), tracers, cols), struct(tracers, LANES)]
        if given:
            outs = outs + [struct(seg * lax.axis_size("lon"), LANES)]
        inputs = [array for part in parts for array in part]
        return call(
            functools.partial(edge_kernel, member, sides, bool(given)),
            (*inputs, states, mix_row, amplitude, step_counts, kron, near, after, *given),
            [ANY, VMEM, VMEM, VMEM, VMEM] * len(sides)
            + [ANY, VMEM, VMEM, SMEM, VMEM, VMEM, ANY] + [VMEM] * len(given),
            [VMEM] * len(outs),
            outs,
            [
                buffer(len(sides), 2, reach + 2, tracers, cols),
                buffer(len(sides), reach, tracers, cols),
                buffer(len(sides), WINDOW, tracers, cols),
                buffer(PLACES, tracers, cols, dtype=BF16),
                buffer(groups, MOST_ROWS, tracers, 4 * LANES, dtype=BF16),
                semaphores(len(sides) * (reach + 1)),
            ],
        )

    a_edges, ae_sums = edge(
        0,
        (True, False),
        ((a_left, a_save_left, *left_statics), (a_right, a_save_right, *right_statics)),
        b_sums,
    )
    bl_resid, bl_sums = edge(-1, (True,), ((b_left, b_save_left, *left_statics),), ae_sums)
    br_resid, _, share = edge(
        -1,
        (False,),
        ((b_right, b_save_right, *right_statics),),
        bl_sums,
        (b_sums, bl_sums, a_sums, ae_sums),
    )
    with jax.named_scope("mean_squares"):
        gathered = lax.all_to_all(share, BOTH, 0, 0, tiled=True)
    scaled, mismatch = call(
        scale_kernel,
        (gathered, bl_resid, b_inner, br_resid, a_edges, a_inner),
        [VMEM] * 6,
        [ANY, VMEM],
        [struct(seg_dev, tracers, n, cols), struct(1, 1)],
        [buffer(seg_dev, n, tracers, cols), semaphores(seg_dev * n)],
    )
    return (scaled, mismatch.reshape(()))


def solution(mesh):
    in_specs = (
        P("seg", None, "lon", None),
        P(),
        P("lon", None),
        P("lon", None),
        P(),
        P(),
        P(),
        P(None, "lon", None),
    )
    out_specs = (P("seg", None, "lon", None), P())
    return jax.shard_map(shards, mesh=mesh, in_specs=in_specs, out_specs=out_specs, check_vma=False)
```
